256 devices in a mesh: frame: 32 (over x, z), head: 8 (over y, core).
Axes of the slice: x: 4, y: 4, z: 8, core: 2. Of those that a mesh axis runs over, the one named last changes fastest.
Arguments:
- queries: bfloat16 [32, 1024, 3072], P('frame', None, 'head'), may hold values from -8 to 8
- keys: bfloat16 [32, 1024, 3072], P('frame', None, 'head'), may hold values from -8 to 8
- values: bfloat16 [32, 1024, 3072], P('frame', None, 'head'), may hold values from -6 to 6
- out_weight: bfloat16 [3072, 3072], P('head'), may hold values from -0.15625 to 0.15625
- head_class: int32 [24], P('head'), may hold values from 0 to 1, as said below
- sink_frame: int32 [24], P('head'), may hold values from 0 to 31
Outputs:
- mixed: bfloat16 [32, 1024, 3072], P('frame', None, 'head')
The draws below stay inside these ranges and needn't reach their ends.
Inputs may be any that keep to these rules, and one draw needn't show every extreme that they name: `head_class`: in each block of 3 consecutive heads, 1 to 2 heads are temporal (1) and the rest spatial (0), so at most 2 are spatial; blocks with 1 and blocks with 2 temporal heads both occur.
All inputs are finite; a program needn't handle non-finite values.
Results may differ from the reference program's by a relative error of at most 0.017.
Values may be sent and summed in bfloat16 or wider, within the bound.
A program may use at most 64 MiB of HBM per device.

```python
import jax
import jax.numpy as jnp
from jax import lax

D = 3072
HEAD_DIM = 128
HEADS_DEV = 3
MAX_TEMP = 2
TOKF = 1024
HEADS = 24
FRAMES = 32
N_HEAD = 8


def noisy_part(key, spread):
    key = jax.random.fold_in(key, spread)
    field = jnp.clip(2.0 * jax.random.normal(key, (FRAMES, TOKF, HEADS, HEAD_DIM), jnp.float32), -8.0, 8.0)
    return field.reshape(FRAMES, TOKF, HEADS * HEAD_DIM).astype(jnp.bfloat16)


def draw_queries(key, part):
    return noisy_part(key, 1)


def draw_keys(key, part):
    return noisy_part(key, 2)


def draw_head_class(key, part):
    key = jax.random.fold_in(key, 11)
    first, second = jax.random.split(key)
    groups = HEADS // HEADS_DEV
    offset = jax.random.randint(first, (), 0, 2)
    counts = 1 + (jnp.arange(groups) + offset) % MAX_TEMP
    scores = jax.random.randint(second, (groups, HEADS_DEV), 0, 1 << 20) * HEADS_DEV + jnp.arange(HEADS_DEV)[None, :]
    ranks = jnp.argsort(jnp.argsort(scores, axis=1), axis=1)
    return (ranks < counts[:, None]).astype(jnp.int32).reshape(HEADS)


def set_ends(entries, own_key, low, largest):
    extent = entries.shape
    spot = [jax.random.randint(jax.random.fold_in(own_key, axis), (), 0, extent[axis]) for axis in range(len(extent))]
    entries = entries.at[tuple(spot)].set(low)
    longest = extent.index(max(extent))
    spot[longest] = (spot[longest] + 1) % extent[longest]
    return entries.at[tuple(spot)].set(largest)


def strengthened(values, key, source, target, blocks, factor):
    def block_of(axis_at):
        return (jnp.arange(values.shape[axis_at]) // (values.shape[axis_at] // blocks)).reshape((-1,) + (1,) * (values.ndim - 1 - axis_at))

    near = jax.random.permutation(key, blocks)[block_of(target)]
    other_side = (block_of(target) + blocks // 2) % blocks
    return jnp.where((block_of(source) == near) | (block_of(source) == other_side), factor * values, values)


def levels(stream_key, shape, cuts, least, top_value):
    def one(dim, shards_of):
        draws = jax.random.uniform(jax.random.fold_in(jax.random.fold_in(stream_key, 6), dim), (shards_of,), jnp.float32, least / len(cuts), top_value / len(cuts))
        return jnp.repeat(jnp.exp(draws), shape[dim] // shards_of).reshape((-1,) + (1,) * (len(shape) - dim - 1))

    gain = one(*cuts[0])
    for cut in cuts[1:]:
        gain = gain * one(*cut)
    return gain


def centred(key, shape, width, bound, shards=(), kind=jnp.bfloat16):
    entries = width * jax.random.normal(key, shape, jnp.float32)
    if shards:
        entries = entries * levels(key, shape, shards, -0.22, 0.18)
    return jnp.clip(entries, -bound, bound).astype(kind)


def bell_draw_with(stream_key, shape, deviation, limit, cuts, heavy, kind=jnp.bfloat16):
    drawn = deviation * jax.random.normal(stream_key, shape, jnp.float32)
    if cuts:
        drawn = drawn * levels(stream_key, shape, cuts, -0.22, 0.18)
    return jnp.clip(strengthened(drawn, jax.random.fold_in(stream_key, 3), *heavy), -limit, limit).astype(kind)


def setup_inputs(seed: int = 0) -> dict:
    seeds = jax.random.split(jax.random.key(seed), 7)
    return {
        "queries": draw_queries(jax.random.fold_in(seeds[6], 71), 0),
        "keys": draw_keys(jax.random.fold_in(seeds[6], 71), 0),
        "values": centred(seeds[2], (FRAMES, TOKF, HEADS * HEAD_DIM), 1.0, 6.0, ((0, 32), (2, 8))),
        "out_weight": bell_draw_with(seeds[3], (HEADS * HEAD_DIM, D), (HEADS * HEAD_DIM) ** -0.5, 0.15625, ((0, 8),), (0, 1, 8, 2.0)),
        "head_class": draw_head_class(jax.random.fold_in(seeds[6], 71), 0),
        "sink_frame": set_ends(jax.random.randint(seeds[5], (HEADS,), 0, FRAMES), jax.random.fold_in(seeds[5], 1), 0, FRAMES - 1).astype(jnp.int32),
    }


def attend(query, keys, values, scale):
    scores = jnp.dot(query, keys.T, preferred_element_type=jnp.float32) * scale
    top = jnp.max(scores, axis=-1, keepdims=True)
    weights = jnp.exp(scores - top)
    total = jnp.sum(weights, axis=-1, keepdims=True)
    mixed = jnp.dot(weights.astype(jnp.bfloat16), values, preferred_element_type=jnp.float32) / total
    return mixed.astype(jnp.bfloat16)


def reference(queries, keys, values, out_weight, head_class, sink_frame):
    scale = HEAD_DIM ** -0.5
    query_four = queries.reshape(FRAMES, TOKF, HEADS, HEAD_DIM)
    keys_four = keys.reshape(FRAMES, TOKF, HEADS, HEAD_DIM)
    values_four = values.reshape(FRAMES, TOKF, HEADS, HEAD_DIM)
    head_ids = jnp.arange(HEADS, dtype=jnp.int32)
    sink_ids = sink_frame.astype(jnp.int32)
    sink_keys = keys_four[sink_ids, :, head_ids, :]
    sink_values = values_four[sink_ids, :, head_ids, :]

    def one_frame(items):
        frame_q, frame_k, frame_v = items
        all_keys = jnp.concatenate([jnp.transpose(frame_k, (1, 0, 2)), sink_keys], axis=1)
        all_values = jnp.concatenate([jnp.transpose(frame_v, (1, 0, 2)), sink_values], axis=1)

        def one_head(head_items):
            head_q, head_k, head_v = head_items
            return attend(head_q, head_k, head_v, scale)

        return lax.map(one_head, (jnp.transpose(frame_q, (1, 0, 2)), all_keys, all_values))

    spatial = jnp.transpose(lax.map(one_frame, (query_four, keys_four, values_four)), (0, 2, 1, 3))

    scores = jnp.einsum("fphd,gphd->phfg", query_four.astype(jnp.float32), keys_four.astype(jnp.float32)) * scale
    top = jnp.max(scores, axis=-1, keepdims=True)
    weights = jnp.exp(scores - top)
    total = jnp.sum(weights, axis=-1)
    rounded = lax.optimization_barrier(weights.astype(jnp.bfloat16)).astype(jnp.float32)
    temporal = jnp.einsum("phfg,gphd->fphd", rounded, values_four.astype(jnp.float32))
    temporal = (temporal / jnp.transpose(total, (2, 0, 1))[..., None]).astype(jnp.bfloat16)

    is_temporal = (head_class == 1)[None, None, :, None]
    combined = jnp.where(is_temporal, temporal, spatial).reshape(FRAMES * TOKF, HEADS * HEAD_DIM)
    grouped = jnp.transpose(combined.reshape(FRAMES * TOKF, N_HEAD, HEADS_DEV * HEAD_DIM), (1, 0, 2))
    weight_groups = out_weight.reshape(N_HEAD, HEADS_DEV * HEAD_DIM, D)

    def add_group(running, items):
        block, weight_block = items
        part = jnp.dot(block, weight_block, preferred_element_type=jnp.float32)
        part = lax.optimization_barrier(part.astype(jnp.bfloat16)).astype(jnp.float32)
        return running + part, None

    summed, unused = lax.scan(add_group, jnp.zeros((FRAMES * TOKF, D), jnp.float32), (grouped, weight_groups))
    return summed.astype(jnp.bfloat16).reshape(FRAMES, TOKF, D)
```

```python
import math

import jax
import jax.numpy as jnp
from jax import lax
from jax.experimental import pallas as pl
from jax.experimental.pallas import tpu as pltpu
from jax.sharding import PartitionSpec as P

MESH = pl.DeviceIdType.MESH
NX, NZ, NY, NC = 4, 8, 4, 2
NF, NH = NX * NZ, NY * NC
TOK, HD, WID = 1024, 128, 384
HALF = TOK // 2
POS = HALF // NF
SLOT_A, SLOT_C, SLOT_B = 0, 1, 2
SCALE = HD ** (-0.5) * math.log2(math.e)


def first_with(cls, kind):
    return jnp.where(cls[0] == kind, 0, jnp.where(cls[1] == kind, 1, 2))


def softmax_times(scores, values):
    top = jnp.max(scores, axis=-1, keepdims=True)
    weights = jnp.exp2((scores - top) * SCALE)
    total = jnp.sum(weights, axis=-1, keepdims=True)
    mixed = jnp.dot(weights.astype(jnp.bfloat16), values, preferred_element_type=jnp.float32)
    return (mixed / total).astype(jnp.bfloat16)


def dot_nt(a, b):
    return lax.dot_general(a, b, (((1,), (1,)), ((), ())), preferred_element_type=jnp.float32)


def kernel(
    cls,
    sink,
    q_hbm,
    k_hbm,
    v_hbm,
    w_hbm,
    out_ref,
    vq,
    vk,
    vv,
    vw,
    xs,
    xr,
    os,
    tc,
    g,
    ws,
    wg,
    acc,
    ss,
    rx,
    qz,
    rz,
    sk,
    kv,
    sc,
    in_sem,
    fs_sem,
    fr_sem,
    bs_sem,
    br_sem,
    ws_sem,
    wr_sem,
    ks_sem,
    kr_sem,
    ys_sem,
    yr_sem,
    cs_sem,
    cr_sem,
):
    f = lax.axis_index("frame")
    h = lax.axis_index("head")
    mx, mz, my, mc = f // NZ, f % NZ, h // NC, h % NC

    ins = []
    for n, (src, dst) in enumerate(((k_hbm, vk), (v_hbm, vv), (q_hbm, vq))):
        for j in range(3):
            cp = pltpu.make_async_copy(
                src.at[0, :, pl.ds(j * HD, HD)], dst.at[j], in_sem.at[n * 3 + j]
            )
            cp.start()
            ins.append(cp)
    for j in range(3):
        cp = pltpu.make_async_copy(w_hbm.at[pl.ds(j * HD, HD)], vw.at[j], in_sem.at[9 + j])
        cp.start()
        ins.append(cp)

    barrier = pltpu.get_barrier_semaphore()

    def greet_frame(d, carry):
        pl.semaphore_signal(
            barrier, inc=1, device_id=(lax.rem(f + d, NF), h), device_id_type=MESH
        )
        return carry

    def greet_head(d, carry):
        pl.semaphore_signal(
            barrier, inc=1, device_id=(f, lax.rem(h + d, NH)), device_id_type=MESH
        )
        return carry

    lax.fori_loop(1, NF, greet_frame, 0)
    lax.fori_loop(1, NH, greet_head, 0)

    ia = first_with(cls, 1)
    ib = first_with(cls, 0)
    ic = 3 - ia - ib
    c_temp = cls[ic] == 1
    head_of = {SLOT_A: ia, SLOT_B: ib, SLOT_C: ic}
    spat = (SLOT_B, SLOT_C)

    for n in range(6):
        ins[n].wait()
    for s, slot in enumerate(spat):
        ss[:, s, 0] = vk[head_of[slot]].reshape(NX, TOK // NX, HD)
        ss[:, s, 1] = vv[head_of[slot]].reshape(NX, TOK // NX, HD)
        kv[s, 0, pl.ds(0, TOK)] = vk[head_of[slot]]
        kv[s, 1, pl.ds(0, TOK)] = vv[head_of[slot]]
    for n in range(6, 9):
        ins[n].wait()
    for slot in (SLOT_A, SLOT_C):
        for half in range(2):
            u = slot * 2 + half
            for t, src in enumerate((vq, vk, vv)):
                part = src[head_of[slot], pl.ds(half * HALF, HALF)]
                xs[u, :, t] = part.reshape(NF, POS, HD)
            xr[u, f] = xs[u, f]
    for n in range(9, 12):
        ins[n].wait()
    for slot in (SLOT_A, SLOT_C, SLOT_B):
        for p in range(NH):
            ws[p, slot] = vw[head_of[slot], :, pl.ds(p * WID, WID)]
    for slot in (SLOT_A, SLOT_C, SLOT_B):
        wg[slot, h] = ws[h, slot]
    for s in range(2):
        rx[mx, s] = ss[mx, s]

    pl.semaphore_wait(barrier, NF - 1 + NH - 1)

    def send_unit(u):
        def one(d, carry):
            p = lax.rem(f + d, NF)
            pltpu.make_async_remote_copy(
                src_ref=xs.at[u, p],
                dst_ref=xr.at[u, f],
                send_sem=fs_sem.at[u],
                recv_sem=fr_sem.at[u],
                device_id=(p, h),
                device_id_type=MESH,
            ).start()
            return carry

        lax.fori_loop(1, NF, one, 0)

    def return_unit(u):
        def one(d, carry):
            p = lax.rem(f + d, NF)
            dst = g.at[SLOT_A, h, u, f] if u < 2 else tc.at[u - 2, f]
            pltpu.make_async_remote_copy(
                src_ref=os.at[u, p],
                dst_ref=dst,
                send_sem=bs_sem.at[u],
                recv_sem=br_sem.at[u],
                device_id=(p, h),
                device_id_type=MESH,
            ).start()
            return carry

        lax.fori_loop(1, NF, one, 0)

    def wait_bytes(ref, sem):
        pltpu.make_async_copy(ref, ref, sem).wait()

    def x_peer(d):
        return lax.rem(mx + d, NX)

    def z_peer(d):
        return lax.rem(mz + d, NZ)

    for d in (1, 3, 2):
        pltpu.make_async_remote_copy(
            src_ref=ss.at[x_peer(d)],
            dst_ref=rx.at[mx],
            send_sem=ks_sem.at[0],
            recv_sem=kr_sem.at[0],
            device_id=(x_peer(d) * NZ + mz, h),
            device_id_type=MESH,
        ).start()
    send_unit(0)

    def send_weights(d, carry):
        p = lax.rem(h + d, NH)
        pltpu.make_async_remote_copy(
            src_ref=ws.at[p],
            dst_ref=wg.at[:, h],
            send_sem=ws_sem,
            recv_sem=wr_sem,
            device_id=(f, p),
            device_id_type=MESH,
        ).start()
        return carry

    lax.fori_loop(1, NH, send_weights, 0)

    root = [sink[head_of[slot]] for slot in spat]
    wait_bytes(rx.at[pl.ds(0, NX - 1)], kr_sem.at[0])
    for s in range(2):
        for t in range(2):
            qz[:, s, t] = rx[root[s] // NZ, s, t].reshape(NZ, TOK // NF, HD)
    rz[mz] = qz[mz]
    for d in (1, 7, 2, 6, 3, 5, 4):
        pltpu.make_async_remote_copy(
            src_ref=qz.at[z_peer(d)],
            dst_ref=rz.at[mz],
            send_sem=ks_sem.at[1],
            recv_sem=kr_sem.at[1],
            device_id=(mx * NZ + z_peer(d), h),
            device_id_type=MESH,
        ).start()
    send_unit(1)
    wait_bytes(rz.at[pl.ds(0, NZ - 1)], kr_sem.at[1])
    for s in range(2):
        sk[mx, mz, s] = rz[root[s] % NZ, s]
    for d in (1, 7, 2, 6, 3, 5, 4):
        pltpu.make_async_remote_copy(
            src_ref=sk.at[mx, mz],
            dst_ref=sk.at[mx, mz],
            send_sem=ks_sem.at[2],
            recv_sem=kr_sem.at[2],
            device_id=(mx * NZ + z_peer(d), h),
            device_id_type=MESH,
        ).start()
    send_unit(2)
    wait_bytes(sk.at[0, pl.ds(0, NZ - 1)], kr_sem.at[2])
    for d in (1, 3, 2):
        pltpu.make_async_remote_copy(
            src_ref=sk.at[mx],
            dst_ref=sk.at[mx],
            send_sem=ks_sem.at[3],
            recv_sem=kr_sem.at[3],
            device_id=(x_peer(d) * NZ + mz, h),
            device_id_type=MESH,
        ).start()
    send_unit(3)

    def temporal(u):
        wait_bytes(xr.at[u, pl.ds(0, NF - 1)], fr_sem.at[u])
        rows = NF * POS
        query = xr[u, :, 0].reshape(rows, HD)
        keys = xr[u, :, 1].reshape(rows, HD)
        values = xr[u, :, 2].reshape(rows, HD)
        scores = dot_nt(query, keys)
        place = lax.broadcasted_iota(jnp.int32, (rows, rows), 0) % POS
        other = lax.broadcasted_iota(jnp.int32, (rows, rows), 1) % POS
        scores = jnp.where(place == other, scores, -1e30)
        os[u] = softmax_times(scores, values).reshape(NF, POS, HD)
        if u < 2:
            g[SLOT_A, h, u, f] = os[u, f]
        else:
            tc[u - 2, f] = os[u, f]
        return_unit(u)

    def gather_y(slot, half):
        n = slot * 2 + half
        for i, d in enumerate((1, 3, 2)):
            p = lax.rem(my + d, NY) * NC + mc
            pltpu.make_async_remote_copy(
                src_ref=g.at[slot, h, half],
                dst_ref=g.at[slot, h, half],
                send_sem=ys_sem.at[n],
                recv_sem=yr_sem.at[n * 3 + i],
                device_id=(f, p),
                device_id_type=MESH,
            ).start()
        core_send(slot, half, h)

    def core_send(slot, half, p):
        n = slot * 2 + half
        pltpu.make_async_remote_copy(
            src_ref=g.at[slot, p, half],
            dst_ref=g.at[slot, p, half],
            send_sem=cs_sem.at[n],
            recv_sem=cr_sem.at[n],
            device_id=(f, my * NC + 1 - mc),
            device_id_type=MESH,
        ).start()

    def gather_core(slot, half):
        n = slot * 2 + half
        for i, d in enumerate((1, 3, 2)):
            p = lax.rem(my + NY - d, NY) * NC + mc
            wait_bytes(g.at[slot, p, half], yr_sem.at[n * 3 + i])
            core_send(slot, half, p)

    def project(slot, half, first, last):
        n = slot * 2 + half
        wait_bytes(g.at[slot, pl.ds(0, NY), half], cr_sem.at[n])
        left = jnp.concatenate([g[slot, p, half].reshape(HALF, HD) for p in range(NH)], axis=1)
        right = wg[slot].reshape(NH * HD, WID)
        part = jnp.dot(left, right, preferred_element_type=jnp.float32)
        rows = pl.ds(half * HALF, HALF)
        if not first:
            part = part + acc[rows]
        if last:
            out_ref[0, rows] = part.astype(jnp.bfloat16)
        else:
            acc[rows] = part

    temporal(0)
    wait_bytes(sk.at[pl.ds(0, NX - 1)], kr_sem.at[3])
    for s in range(2):
        for t in range(2):
            kv[s, t, pl.ds(TOK, TOK)] = sk[:, :, s, t].reshape(TOK, HD)

    block = 256

    def spatial(s, n):
        query = vq[head_of[spat[s]], pl.ds(pl.multiple_of(n * block, block), block)]
        return softmax_times(dot_nt(query, kv[s, 0]), kv[s, 1])

    per = block // POS

    def spatial_b(n, carry):
        half = n // (HALF // block)
        at = n % (HALF // block)
        g[SLOT_B, h, half, pl.ds(at * per, per)] = spatial(0, n).reshape(per, POS, HD)
        return carry

    def spatial_c(n, carry):
        half = n // (HALF // block)
        at = n % (HALF // block)
        sc[half, pl.ds(at * per, per)] = spatial(1, n).reshape(per, POS, HD)
        return carry

    lax.fori_loop(0, TOK // block, spatial_b, 0)
    gather_y(SLOT_B, 0)
    gather_y(SLOT_B, 1)
    lax.fori_loop(0, TOK // block, spatial_c, 0)

    def back_a(half):
        wait_bytes(g.at[SLOT_A, h, half, pl.ds(0, NF - 1)], br_sem.at[half])
        gather_y(SLOT_A, half)

    def back_c(half):
        wait_bytes(tc.at[half, pl.ds(0, NF - 1)], br_sem.at[2 + half])
        g[SLOT_C, h, half] = jnp.where(c_temp, tc[half], sc[half])
        gather_y(SLOT_C, half)

    temporal(1)
    back_a(0)
    gather_core(SLOT_B, 0)
    gather_core(SLOT_B, 1)
    temporal(2)
    back_a(1)
    temporal(3)
    gather_core(SLOT_A, 0)
    wait_bytes(wg.at[:, pl.ds(0, NH - 1)], wr_sem)
    back_c(0)
    project(SLOT_B, 0, True, False)
    project(SLOT_B, 1, True, False)
    gather_core(SLOT_A, 1)
    back_c(1)
    project(SLOT_A, 0, False, False)
    project(SLOT_A, 1, False, False)
    gather_core(SLOT_C, 0)
    gather_core(SLOT_C, 1)
    project(SLOT_C, 0, False, True)
    project(SLOT_C, 1, False, True)

    for u in range(4):
        wait_bytes(xs.at[u, pl.ds(0, NF - 1)], fs_sem.at[u])
        wait_bytes(os.at[u, pl.ds(0, NF - 1)], bs_sem.at[u])
    wait_bytes(ws.at[pl.ds(0, NH - 1)], ws_sem)
    wait_bytes(ss.at[pl.ds(0, NX - 1)], ks_sem.at[0])
    wait_bytes(qz.at[pl.ds(0, NZ - 1)], ks_sem.at[1])
    wait_bytes(sk.at[0, pl.ds(0, NZ - 1)], ks_sem.at[2])
    wait_bytes(sk.at[pl.ds(0, NX - 1)], ks_sem.at[3])
    for n in range(6):
        wait_bytes(g.at[0, pl.ds(0, NY - 1), 0], ys_sem.at[n])
        wait_bytes(g.at[0, pl.ds(0, NY), 0], cs_sem.at[n])


def per_device(queries, keys, values, out_weight, head_class, sink_frame):
    bf16, f32 = jnp.bfloat16, jnp.float32
    dma = pltpu.SemaphoreType.DMA
    spread = pltpu.VMEM
    return pl.pallas_call(
        kernel,
        out_shape=jax.ShapeDtypeStruct((1, TOK, WID), bf16),
        in_specs=[pl.BlockSpec(memory_space=pltpu.SMEM)] * 2
        + [pl.BlockSpec(memory_space=pl.ANY)] * 4,
        out_specs=pl.BlockSpec(memory_space=pltpu.VMEM),
        scratch_shapes=[
            spread((3, TOK, HD), bf16),
            spread((3, TOK, HD), bf16),
            spread((3, TOK, HD), bf16),
            spread((3, HD, NH * WID), bf16),
            spread((4, NF, 3, POS, HD), bf16),
            spread((4, NF, 3, POS, HD), bf16),
            spread((4, NF, POS, HD), bf16),
            spread((2, NF, POS, HD), bf16),
            spread((3, NH, 2, NF, POS, HD), bf16),
            spread((NH, 3, HD, WID), bf16),
            spread((3, NH, HD, WID), bf16),
            spread((TOK, WID), f32),
            spread((NX, 2, 2, TOK // NX, HD), bf16),
            spread((NX, 2, 2, TOK // NX, HD), bf16),
            spread((NZ, 2, 2, TOK // NF, HD), bf16),
            spread((NZ, 2, 2, TOK // NF, HD), bf16),
            spread((NX, NZ, 2, 2, TOK // NF, HD), bf16),
            spread((2, 2, 2 * TOK, HD), bf16),
            spread((2, NF, POS, HD), bf16),
            dma((12,)),
            dma((4,)),
            dma((4,)),
            dma((4,)),
            dma((4,)),
            dma,
            dma,
            dma((4,)),
            dma((4,)),
            dma((6,)),
            dma((18,)),
            dma((6,)),
            dma((6,)),
        ],
        compiler_params=pltpu.CompilerParams(
            collective_id=0, has_side_effects=True, vmem_limit_bytes=56 * 2**20
        ),
        cost_estimate=pl.CostEstimate(
            flops=7 * 10**9, bytes_accessed=8 * 10**6, transcendentals=6 * 10**6
        ),
    )(head_class, sink_frame, queries, keys, values, out_weight)


def solution(mesh):
    placed = (
        P("frame", None, "head"),
        P("frame", None, "head"),
        P("frame", None, "head"),
        P("head", None),
        P("head"),
        P("head"),
    )
    return jax.shard_map(
        per_device, mesh=mesh, in_specs=placed, out_specs=P("frame", None, "head"), check_vma=False
    )
```

```python
import math

import jax
import jax.numpy as jnp
from jax import lax
from jax.experimental import pallas as pl
from jax.experimental.pallas import tpu as pltpu
from jax.sharding import PartitionSpec as P

MESH = pl.DeviceIdType.MESH
NX, NZ, NY, NC = 4, 8, 4, 2
NF, NH = NX * NZ, NY * NC
TOK, HD, WID = 1024, 128, 384
HALF = TOK // 2
POS = HALF // NF
SLOT_A, SLOT_C, SLOT_B = 0, 1, 2
SCALE = HD ** (-0.5) * math.log2(math.e)


def first_with(cls, kind):
    return jnp.where(cls[0] == kind, 0, jnp.where(cls[1] == kind, 1, 2))


def softmax_times(scores, values):
    top = jnp.max(scores, axis=-1, keepdims=True)
    weights = jnp.exp2((scores - top) * SCALE)
    total = jnp.sum(weights, axis=-1, keepdims=True)
    mixed = jnp.dot(weights.astype(jnp.bfloat16), values, preferred_element_type=jnp.float32)
    return (mixed / total).astype(jnp.bfloat16)


def dot_nt(a, b):
    return lax.dot_general(a, b, (((1,), (1,)), ((), ())), preferred_element_type=jnp.float32)


def kernel(
    cls,
    sink,
    q_hbm,
    k_hbm,
    v_hbm,
    w_hbm,
    out_ref,
    vq,
    vk,
    vv,
    vw,
    xa,
    ra,
    xk,
    rk,
    xq,
    rq,
    os,
    tc,
    g,
    ws,
    wg,
    acc,
    ss,
    rx,
    qz,
    rz,
    sk,
    kv,
    sc,
    in_sem,
    fs_sem,
    fr_sem,
    bs_sem,
    br_sem,
    ws_sem,
    wr_sem,
    ks_sem,
    kr_sem,
    ys_sem,
    yr_sem,
    cs_sem,
    cr_sem,
):
    f = lax.axis_index("frame")
    h = lax.axis_index("head")
    mx, mz, my, mc = f // NZ, f % NZ, h // NC, h % NC

    ins = []
    for n, (src, dst) in enumerate(((k_hbm, vk), (v_hbm, vv), (q_hbm, vq))):
        for j in range(3):
            cp = pltpu.make_async_copy(
                src.at[0, :, pl.ds(j * HD, HD)], dst.at[j], in_sem.at[n * 3 + j]
            )
            cp.start()
            ins.append(cp)
    for j in range(3):
        cp = pltpu.make_async_copy(w_hbm.at[pl.ds(j * HD, HD)], vw.at[j], in_sem.at[9 + j])
        cp.start()
        ins.append(cp)

    barrier = pltpu.get_barrier_semaphore()

    def greet_frame(d, carry):
        pl.semaphore_signal(
            barrier, inc=1, device_id=(lax.rem(f + d, NF), h), device_id_type=MESH
        )
        return carry

    def greet_head(d, carry):
        pl.semaphore_signal(
            barrier, inc=1, device_id=(f, lax.rem(h + d, NH)), device_id_type=MESH
        )
        return carry

    lax.fori_loop(1, NF, greet_frame, 0)
    lax.fori_loop(1, NH, greet_head, 0)

    ia = first_with(cls, 1)
    ib = first_with(cls, 0)
    ic = 3 - ia - ib
    c_temp = cls[ic] == 1
    head_of = {SLOT_A: ia, SLOT_B: ib, SLOT_C: ic}
    spat = (SLOT_B, SLOT_C)
    root_b, root_c = sink[ib], sink[ic]

    def wait_bytes(ref, sem):
        pltpu.make_async_copy(ref, ref, sem).wait()

    def x_peer(d):
        return lax.rem(mx + d, NX)

    def z_peer(d):
        return lax.rem(mz + d, NZ)

    def to_frames(src, dst, send_sem, recv_sem):
        def one(d, carry):
            p = lax.rem(f + d, NF)
            pltpu.make_async_remote_copy(
                src_ref=src.at[p],
                dst_ref=dst,
                send_sem=send_sem,
                recv_sem=recv_sem,
                device_id=(p, h),
                device_id_type=MESH,
            ).start()
            return carry

        lax.fori_loop(1, NF, one, 0)

    def to_x(src, dst, n):
        for d in (1, 3, 2):
            pltpu.make_async_remote_copy(
                src_ref=src(x_peer(d)),
                dst_ref=dst,
                send_sem=ks_sem.at[n],
                recv_sem=kr_sem.at[n],
                device_id=(x_peer(d) * NZ + mz, h),
                device_id_type=MESH,
            ).start()

    def to_z(src, dst, n):
        for d in (1, 7, 2, 6, 3, 5, 4):
            pltpu.make_async_remote_copy(
                src_ref=src(z_peer(d)),
                dst_ref=dst,
                send_sem=ks_sem.at[n],
                recv_sem=kr_sem.at[n],
                device_id=(mx * NZ + z_peer(d), h),
                device_id_type=MESH,
            ).start()

    for n in range(6):
        ins[n].wait()
    ss[:, 0] = vk[ib].reshape(NX, TOK // NX, HD)
    ss[:, 1] = vv[ib].reshape(NX, TOK // NX, HD)
    for t, src in enumerate((vk, vv)):
        for half in range(2):
            xk[:, t, half] = src[ic, pl.ds(half * HALF, HALF)].reshape(NF, POS, HD)
    pl.semaphore_wait(barrier, NF - 1 + NH - 1)
    to_x(lambda p: ss.at[p], rx.at[mx], 0)
    rx[mx] = ss[mx]
    rk[f] = xk[f]

    for n in range(9, 12):
        ins[n].wait()
    for slot in (SLOT_A, SLOT_C, SLOT_B):
        for p in range(NH):
            ws[p, slot] = vw[head_of[slot], :, pl.ds(p * WID, WID)]
        wg[slot, h] = ws[h, slot]

    def send_weights(d, carry):
        p = lax.rem(h + d, NH)
        pltpu.make_async_remote_copy(
            src_ref=ws.at[p],
            dst_ref=wg.at[:, h],
            send_sem=ws_sem,
            recv_sem=wr_sem,
            device_id=(f, p),
            device_id_type=MESH,
        ).start()
        return carry

    lax.fori_loop(1, NH, send_weights, 0)
    to_frames(xk, rk.at[f], fs_sem.at[2], fr_sem.at[2])

    for n in range(6, 9):
        ins[n].wait()
    for half in range(2):
        for t, src in enumerate((vq, vk, vv)):
            xa[half, :, t] = src[ia, pl.ds(half * HALF, HALF)].reshape(NF, POS, HD)
        ra[half, f] = xa[half, f]
        xq[half] = vq[ic, pl.ds(half * HALF, HALF)].reshape(NF, POS, HD)
        rq[half, f] = xq[half, f]
    for s, slot in enumerate(spat):
        kv[s, 0, pl.ds(0, TOK)] = vk[head_of[slot]]
        kv[s, 1, pl.ds(0, TOK)] = vv[head_of[slot]]

    def send_a(half):
        to_frames(xa.at[half], ra.at[half, f], fs_sem.at[half], fr_sem.at[half])

    def send_q(half):
        to_frames(xq.at[half], rq.at[half, f], fs_sem.at[3 + half], fr_sem.at[3 + half])

    wait_bytes(rx.at[pl.ds(0, NX - 1)], kr_sem.at[0])
    for t in range(2):
        qz[:, t] = rx[root_b // NZ, t].reshape(NZ, TOK // NF, HD)
    rz[mz] = qz[mz]
    to_z(lambda p: qz.at[p], rz.at[mz], 1)
    wait_bytes(rz.at[pl.ds(0, NZ - 1)], kr_sem.at[1])
    sk[0, mx, mz] = rz[root_b % NZ]
    to_z(lambda p: sk.at[0, mx, mz], sk.at[0, mx, mz], 2)
    wait_bytes(rk.at[pl.ds(0, NF - 1)], fr_sem.at[2])
    sk[1, mx, mz] = rk[root_c].reshape(2, 2 * POS, HD)
    to_z(lambda p: sk.at[1, mx, mz], sk.at[1, mx, mz], 3)
    send_a(0)
    wait_bytes(sk.at[0, 0, pl.ds(0, NZ - 1)], kr_sem.at[2])
    to_x(lambda p: sk.at[0, mx], sk.at[0, mx], 4)
    wait_bytes(sk.at[1, 0, pl.ds(0, NZ - 1)], kr_sem.at[3])
    to_x(lambda p: sk.at[1, mx], sk.at[1, mx], 5)
    send_a(1)

    def attend_positions(query, keys, values, u):
        rows = NF * POS
        query, keys, values = (a.reshape(rows, HD) for a in (query, keys, values))
        scores = dot_nt(query, keys)
        place = lax.broadcasted_iota(jnp.int32, (rows, rows), 0) % POS
        other = lax.broadcasted_iota(jnp.int32, (rows, rows), 1) % POS
        scores = jnp.where(place == other, scores, -1e30)
        os[u] = softmax_times(scores, values).reshape(NF, POS, HD)

    def temporal_a(half):
        wait_bytes(ra.at[half, pl.ds(0, NF - 1)], fr_sem.at[half])
        attend_positions(ra[half, :, 0], ra[half, :, 1], ra[half, :, 2], half)
        g[SLOT_A, h, half, f] = os[half, f]
        to_frames(os.at[half], g.at[SLOT_A, h, half, f], bs_sem.at[half], br_sem.at[half])

    def temporal_c(half):
        wait_bytes(rq.at[half, pl.ds(0, NF - 1)], fr_sem.at[3 + half])
        attend_positions(rq[half], rk[:, 0, half], rk[:, 1, half], 2 + half)
        tc[half, f] = os[2 + half, f]
        to_frames(os.at[2 + half], tc.at[half, f], bs_sem.at[2 + half], br_sem.at[2 + half])

    def core_send(slot, half, p):
        n = slot * 2 + half
        pltpu.make_async_remote_copy(
            src_ref=g.at[slot, p, half],
            dst_ref=g.at[slot, p, half],
            send_sem=cs_sem.at[n],
            recv_sem=cr_sem.at[n],
            device_id=(f, my * NC + 1 - mc),
            device_id_type=MESH,
        ).start()

    up = lax.rem(my + 1, NY) * NC + mc
    down = lax.rem(my + NY - 1, NY) * NC + mc
    across = lax.rem(my + 2, NY) * NC + mc

    def y_send(ref, n, i, p):
        pltpu.make_async_remote_copy(
            src_ref=ref,
            dst_ref=ref,
            send_sem=ys_sem.at[n],
            recv_sem=yr_sem.at[n * 3 + i],
            device_id=(f, p),
            device_id_type=MESH,
        ).start()

    def gather_y(slot, half):
        n = slot * 2 + half
        y_send(g.at[slot, h, half], n, 0, up)
        y_send(g.at[slot, h, half], n, 1, down)
        core_send(slot, half, h)

    def pass_on(slot, half):
        n = slot * 2 + half
        wait_bytes(g.at[slot, down, half], yr_sem.at[n * 3])
        y_send(g.at[slot, down, half, pl.ds(0, NF // 2)], n, 2, up)
        core_send(slot, half, down)
        wait_bytes(g.at[slot, up, half], yr_sem.at[n * 3 + 1])
        y_send(g.at[slot, up, half, pl.ds(NF // 2, NF // 2)], n, 2, down)
        core_send(slot, half, up)

    def gather_core(slot, half):
        n = slot * 2 + half
        wait_bytes(g.at[slot, across, half], yr_sem.at[n * 3 + 2])
        core_send(slot, half, across)

    def project(slot, half, first, last):
        n = slot * 2 + half
        wait_bytes(g.at[slot, pl.ds(0, NY), half], cr_sem.at[n])
        left = jnp.concatenate([g[slot, p, half].reshape(HALF, HD) for p in range(NH)], axis=1)
        right = wg[slot].reshape(NH * HD, WID)
        part = jnp.dot(left, right, preferred_element_type=jnp.float32)
        rows = pl.ds(half * HALF, HALF)
        if not first:
            part = part + acc[rows]
        if last:
            out_ref[0, rows] = part.astype(jnp.bfloat16)
        else:
            acc[rows] = part

    block = 256
    per = block // POS

    def spatial(s, n):
        query = vq[head_of[spat[s]], pl.ds(pl.multiple_of(n * block, block), block)]
        return softmax_times(dot_nt(query, kv[s, 0]), kv[s, 1]).reshape(per, POS, HD)

    def spatial_b(half):
        def one(n, carry):
            g[SLOT_B, h, half, pl.ds(n * per, per)] = spatial(0, half * (HALF // block) + n)
            return carry

        lax.fori_loop(0, HALF // block, one, 0)

    def spatial_c(half):
        def one(n, carry):
            sc[half, pl.ds(n * per, per)] = spatial(1, half * (HALF // block) + n)
            return carry

        lax.fori_loop(0, HALF // block, one, 0)

    def back_a(half):
        wait_bytes(g.at[SLOT_A, h, half, pl.ds(0, NF - 1)], br_sem.at[half])
        gather_y(SLOT_A, half)

    def back_c(half):
        wait_bytes(tc.at[half, pl.ds(0, NF - 1)], br_sem.at[2 + half])
        g[SLOT_C, h, half] = jnp.where(c_temp, tc[half], sc[half])
        gather_y(SLOT_C, half)

    def sink_ready(s):
        wait_bytes(sk.at[s, pl.ds(0, NX - 1)], kr_sem.at[4 + s])
        for t in range(2):
            kv[s, t, pl.ds(TOK, TOK)] = sk[s, :, :, t].reshape(TOK, HD)

    temporal_a(0)
    send_q(0)
    send_q(1)
    sink_ready(0)
    spatial_b(0)
    gather_y(SLOT_B, 0)
    spatial_b(1)
    gather_y(SLOT_B, 1)
    temporal_a(1)
    back_a(0)
    sink_ready(1)
    spatial_c(0)
    pass_on(SLOT_B, 0)
    spatial_c(1)
    pass_on(SLOT_B, 1)
    temporal_c(0)
    gather_core(SLOT_B, 0)
    temporal_c(1)
    pass_on(SLOT_A, 0)
    gather_core(SLOT_B, 1)
    back_a(1)
    gather_core(SLOT_A, 0)
    back_c(0)
    pass_on(SLOT_A, 1)
    wait_bytes(wg.at[:, pl.ds(0, NH - 1)], wr_sem)
    project(SLOT_B, 0, True, False)
    back_c(1)
    pass_on(SLOT_C, 0)
    gather_core(SLOT_A, 1)
    project(SLOT_A, 0, False, False)
    pass_on(SLOT_C, 1)
    gather_core(SLOT_C, 0)
    project(SLOT_B, 1, True, False)
    gather_core(SLOT_C, 1)
    project(SLOT_A, 1, False, False)
    project(SLOT_C, 0, False, True)
    project(SLOT_C, 1, False, True)

    for half in range(2):
        wait_bytes(xa.at[half, pl.ds(0, NF - 1)], fs_sem.at[half])
        wait_bytes(xq.at[half, pl.ds(0, NF - 1)], fs_sem.at[3 + half])
    wait_bytes(xk.at[pl.ds(0, NF - 1)], fs_sem.at[2])
    for u in range(4):
        wait_bytes(os.at[u, pl.ds(0, NF - 1)], bs_sem.at[u])
    wait_bytes(ws.at[pl.ds(0, NH - 1)], ws_sem)
    wait_bytes(ss.at[pl.ds(0, NX - 1)], ks_sem.at[0])
    wait_bytes(qz.at[pl.ds(0, NZ - 1)], ks_sem.at[1])
    for s in range(2):
        wait_bytes(sk.at[s, 0, pl.ds(0, NZ - 1)], ks_sem.at[2 + s])
        wait_bytes(sk.at[s, pl.ds(0, NX - 1)], ks_sem.at[4 + s])
    for n in range(6):
        wait_bytes(g.at[0, pl.ds(0, NY - 1), 0], ys_sem.at[n])
        wait_bytes(g.at[0, pl.ds(0, NY), 0], cs_sem.at[n])


def per_device(queries, keys, values, out_weight, head_class, sink_frame):
    bf16, f32 = jnp.bfloat16, jnp.float32
    dma = pltpu.SemaphoreType.DMA
    spread = pltpu.VMEM
    return pl.pallas_call(
        kernel,
        out_shape=jax.ShapeDtypeStruct((1, TOK, WID), bf16),
        in_specs=[pl.BlockSpec(memory_space=pltpu.SMEM)] * 2
        + [pl.BlockSpec(memory_space=pl.ANY)] * 4,
        out_specs=pl.BlockSpec(memory_space=pltpu.VMEM),
        scratch_shapes=[
            spread((3, TOK, HD), bf16),
            spread((3, TOK, HD), bf16),
            spread((3, TOK, HD), bf16),
            spread((3, HD, NH * WID), bf16),
            spread((2, NF, 3, POS, HD), bf16),
            spread((2, NF, 3, POS, HD), bf16),
            spread((NF, 2, 2, POS, HD), bf16),
            spread((NF, 2, 2, POS, HD), bf16),
            spread((2, NF, POS, HD), bf16),
            spread((2, NF, POS, HD), bf16),
            spread((4, NF, POS, HD), bf16),
            spread((2, NF, POS, HD), bf16),
            spread((3, NH, 2, NF, POS, HD), bf16),
            spread((NH, 3, HD, WID), bf16),
            spread((3, NH, HD, WID), bf16),
            spread((TOK, WID), f32),
            spread((NX, 2, TOK // NX, HD), bf16),
            spread((NX, 2, TOK // NX, HD), bf16),
            spread((NZ, 2, TOK // NF, HD), bf16),
            spread((NZ, 2, TOK // NF, HD), bf16),
            spread((2, NX, NZ, 2, TOK // NF, HD), bf16),
            spread((2, 2, 2 * TOK, HD), bf16),
            spread((2, NF, POS, HD), bf16),
            dma((12,)),
            dma((5,)),
            dma((5,)),
            dma((4,)),
            dma((4,)),
            dma,
            dma,
            dma((6,)),
            dma((6,)),
            dma((6,)),
            dma((18,)),
            dma((6,)),
            dma((6,)),
        ],
        compiler_params=pltpu.CompilerParams(
            collective_id=0, has_side_effects=True, vmem_limit_bytes=56 * 2**20
        ),
        cost_estimate=pl.CostEstimate(
            flops=7 * 10**9, bytes_accessed=8 * 10**6, transcendentals=6 * 10**6
        ),
    )(head_class, sink_frame, queries, keys, values, out_weight)


def solution(mesh):
    placed = (
        P("frame", None, "head"),
        P("frame", None, "head"),
        P("frame", None, "head"),
        P("head", None),
        P("head"),
        P("head"),
    )
    return jax.shard_map(
        per_device, mesh=mesh, in_specs=placed, out_specs=P("frame", None, "head"), check_vma=False
    )
```

```python
import math

import jax
import jax.numpy as jnp
from jax import lax
from jax.experimental import pallas as pl
from jax.experimental.pallas import tpu as pltpu
from jax.sharding import PartitionSpec as P

MESH = pl.DeviceIdType.MESH
NX, NZ, NY, NC = 4, 8, 4, 2
NF, NH = NX * NZ, NY * NC
TOK, HD, WID = 1024, 128, 384
HALF = TOK // 2
POS = HALF // NF
SLOT_A, SLOT_C, SLOT_B = 0, 1, 2
SCALE = HD ** (-0.5) * math.log2(math.e)


def first_with(cls, kind):
    return jnp.where(cls[0] == kind, 0, jnp.where(cls[1] == kind, 1, 2))


def softmax_times(scores, values):
    top = jnp.max(scores, axis=-1, keepdims=True)
    weights = jnp.exp2((scores - top) * SCALE)
    total = jnp.sum(weights, axis=-1, keepdims=True)
    mixed = jnp.dot(weights.astype(jnp.bfloat16), values, preferred_element_type=jnp.float32)
    return (mixed / total).astype(jnp.bfloat16)


def dot_nt(a, b):
    return lax.dot_general(a, b, (((1,), (1,)), ((), ())), preferred_element_type=jnp.float32)


def kernel(
    cls,
    sink,
    q_hbm,
    k_hbm,
    v_hbm,
    w_hbm,
    out_ref,
    vq,
    vk,
    vv,
    vw,
    xa,
    ra,
    xk,
    rk,
    xq,
    rq,
    os,
    tc,
    g,
    ws,
    wg,
    acc,
    ss,
    rx,
    qz,
    rz,
    sk,
    kv,
    sc,
    in_sem,
    fs_sem,
    fr_sem,
    bs_sem,
    br_sem,
    ws_sem,
    wr_sem,
    ks_sem,
    kr_sem,
    ys_sem,
    yr_sem,
    cs_sem,
    cr_sem,
):
    f = lax.axis_index("frame")
    h = lax.axis_index("head")
    mx, mz, my, mc = f // NZ, f % NZ, h // NC, h % NC

    ins = []
    for n, (src, dst) in enumerate(((k_hbm, vk), (v_hbm, vv), (q_hbm, vq))):
        for j in range(3):
            cp = pltpu.make_async_copy(
                src.at[0, :, pl.ds(j * HD, HD)], dst.at[j], in_sem.at[n * 3 + j]
            )
            cp.start()
            ins.append(cp)
    for j in range(3):
        cp = pltpu.make_async_copy(w_hbm.at[pl.ds(j * HD, HD)], vw.at[j], in_sem.at[9 + j])
        cp.start()
        ins.append(cp)

    barrier = pltpu.get_barrier_semaphore()

    def greet_frame(d, carry):
        pl.semaphore_signal(
            barrier, inc=1, device_id=(lax.rem(f + d, NF), h), device_id_type=MESH
        )
        return carry

    def greet_head(d, carry):
        pl.semaphore_signal(
            barrier, inc=1, device_id=(f, lax.rem(h + d, NH)), device_id_type=MESH
        )
        return carry

    lax.fori_loop(1, NF, greet_frame, 0)
    lax.fori_loop(1, NH, greet_head, 0)

    ia = first_with(cls, 1)
    ib = first_with(cls, 0)
    ic = 3 - ia - ib
    c_temp = cls[ic] == 1
    head_of = {SLOT_A: ia, SLOT_B: ib, SLOT_C: ic}
    spat = (SLOT_B, SLOT_C)
    root_b, root_c = sink[ib], sink[ic]

    def wait_bytes(ref, sem):
        pltpu.make_async_copy(ref, ref, sem).wait()

    def x_peer(d):
        return lax.rem(mx + d, NX)

    def z_peer(d):
        return lax.rem(mz + d, NZ)

    def to_frames(src, dst, send_sem, recv_sem):
        def one(d, carry):
            p = lax.rem(f + lax.rem(d, 2) * ((d + 1) // 2) + (1 - lax.rem(d, 2)) * (NF - d // 2), NF)
            pltpu.make_async_remote_copy(
                src_ref=src.at[p],
                dst_ref=dst,
                send_sem=send_sem,
                recv_sem=recv_sem,
                device_id=(p, h),
                device_id_type=MESH,
            ).start()
            return carry

        lax.fori_loop(1, NF, one, 0)

    def to_x(src, dst, n):
        for d in (1, 3, 2):
            pltpu.make_async_remote_copy(
                src_ref=src(x_peer(d)),
                dst_ref=dst,
                send_sem=ks_sem.at[n],
                recv_sem=kr_sem.at[n],
                device_id=(x_peer(d) * NZ + mz, h),
                device_id_type=MESH,
            ).start()

    def to_z(src, dst, n):
        for d in (1, 7, 2, 6, 3, 5, 4):
            pltpu.make_async_remote_copy(
                src_ref=src(z_peer(d)),
                dst_ref=dst,
                send_sem=ks_sem.at[n],
                recv_sem=kr_sem.at[n],
                device_id=(mx * NZ + z_peer(d), h),
                device_id_type=MESH,
            ).start()

    for n in range(6):
        ins[n].wait()
    ss[:, 0] = vk[ib].reshape(NX, TOK // NX, HD)
    ss[:, 1] = vv[ib].reshape(NX, TOK // NX, HD)
    for t, src in enumerate((vk, vv)):
        for half in range(2):
            xk[:, t, half] = src[ic, pl.ds(half * HALF, HALF)].reshape(NF, POS, HD)
    pl.semaphore_wait(barrier, NF - 1 + NH - 1)
    to_x(lambda p: ss.at[p], rx.at[mx], 0)
    rx[mx] = ss[mx]
    rk[f] = xk[f]

    for n in range(9, 12):
        ins[n].wait()
    for slot in (SLOT_A, SLOT_C, SLOT_B):
        for p in range(NH):
            ws[p, slot] = vw[head_of[slot], :, pl.ds(p * WID, WID)]
        wg[slot, h] = ws[h, slot]

    def send_weights(d, carry):
        p = lax.rem(h + d, NH)
        pltpu.make_async_remote_copy(
            src_ref=ws.at[p],
            dst_ref=wg.at[:, h],
            send_sem=ws_sem,
            recv_sem=wr_sem,
            device_id=(f, p),
            device_id_type=MESH,
        ).start()
        return carry

    lax.fori_loop(1, NH, send_weights, 0)
    to_frames(xk, rk.at[f], fs_sem.at[2], fr_sem.at[2])

    for n in range(6, 9):
        ins[n].wait()
    for half in range(2):
        for t, src in enumerate((vq, vk, vv)):
            xa[half, :, t] = src[ia, pl.ds(half * HALF, HALF)].reshape(NF, POS, HD)
        ra[half, f] = xa[half, f]
        xq[half] = vq[ic, pl.ds(half * HALF, HALF)].reshape(NF, POS, HD)
        rq[half, f] = xq[half, f]
    for s, slot in enumerate(spat):
        kv[s, 0, pl.ds(0, TOK)] = vk[head_of[slot]]
        kv[s, 1, pl.ds(0, TOK)] = vv[head_of[slot]]

    def send_a(half):
        to_frames(xa.at[half], ra.at[half, f], fs_sem.at[half], fr_sem.at[half])

    def send_q(half):
        to_frames(xq.at[half], rq.at[half, f], fs_sem.at[3 + half], fr_sem.at[3 + half])

    wait_bytes(rx.at[pl.ds(0, NX - 1)], kr_sem.at[0])
    for t in range(2):
        qz[:, t] = rx[root_b // NZ, t].reshape(NZ, TOK // NF, HD)
    rz[mz] = qz[mz]
    to_z(lambda p: qz.at[p], rz.at[mz], 1)
    wait_bytes(rz.at[pl.ds(0, NZ - 1)], kr_sem.at[1])
    sk[0, mx, mz] = rz[root_b % NZ]
    to_z(lambda p: sk.at[0, mx, mz], sk.at[0, mx, mz], 2)
    wait_bytes(rk.at[pl.ds(0, NF - 1)], fr_sem.at[2])
    sk[1, mx, mz] = rk[root_c].reshape(2, 2 * POS, HD)
    to_z(lambda p: sk.at[1, mx, mz], sk.at[1, mx, mz], 3)
    send_a(0)
    wait_bytes(sk.at[0, 0, pl.ds(0, NZ - 1)], kr_sem.at[2])
    to_x(lambda p: sk.at[0, mx], sk.at[0, mx], 4)
    wait_bytes(sk.at[1, 0, pl.ds(0, NZ - 1)], kr_sem.at[3])
    to_x(lambda p: sk.at[1, mx], sk.at[1, mx], 5)
    send_a(1)

    def attend_positions(query, keys, values, u):
        rows = NF * POS
        query, keys, values = (a.reshape(rows, HD) for a in (query, keys, values))
        scores = dot_nt(query, keys)
        place = lax.broadcasted_iota(jnp.int32, (rows, rows), 0) % POS
        other = lax.broadcasted_iota(jnp.int32, (rows, rows), 1) % POS
        scores = jnp.where(place == other, scores, -1e30)
        os[u] = softmax_times(scores, values).reshape(NF, POS, HD)

    def temporal_a(half):
        wait_bytes(ra.at[half, pl.ds(0, NF - 1)], fr_sem.at[half])
        attend_positions(ra[half, :, 0], ra[half, :, 1], ra[half, :, 2], half)
        g[SLOT_A, h, half, f] = os[half, f]
        to_frames(os.at[half], g.at[SLOT_A, h, half, f], bs_sem.at[half], br_sem.at[half])

    def temporal_c(half):
        wait_bytes(rq.at[half, pl.ds(0, NF - 1)], fr_sem.at[3 + half])
        attend_positions(rq[half], rk[:, 0, half], rk[:, 1, half], 2 + half)
        tc[half, f] = os[2 + half, f]
        to_frames(os.at[2 + half], tc.at[half, f], bs_sem.at[2 + half], br_sem.at[2 + half])

    def core_send(slot, half, p):
        n = slot * 2 + half
        pltpu.make_async_remote_copy(
            src_ref=g.at[slot, p, half],
            dst_ref=g.at[slot, p, half],
            send_sem=cs_sem.at[n],
            recv_sem=cr_sem.at[n],
            device_id=(f, my * NC + 1 - mc),
            device_id_type=MESH,
        ).start()

    up = lax.rem(my + 1, NY) * NC + mc
    down = lax.rem(my + NY - 1, NY) * NC + mc
    across = lax.rem(my + 2, NY) * NC + mc

    def y_send(ref, n, i, p):
        pltpu.make_async_remote_copy(
            src_ref=ref,
            dst_ref=ref,
            send_sem=ys_sem.at[n],
            recv_sem=yr_sem.at[n * 3 + i],
            device_id=(f, p),
            device_id_type=MESH,
        ).start()

    def gather_y(slot, half):
        n = slot * 2 + half
        y_send(g.at[slot, h, half], n, 0, up)
        y_send(g.at[slot, h, half], n, 1, down)
        core_send(slot, half, h)

    def pass_on(slot, half):
        n = slot * 2 + half
        wait_bytes(g.at[slot, down, half], yr_sem.at[n * 3])
        y_send(g.at[slot, down, half, pl.ds(0, NF // 2)], n, 2, up)
        core_send(slot, half, down)
        wait_bytes(g.at[slot, up, half], yr_sem.at[n * 3 + 1])
        y_send(g.at[slot, up, half, pl.ds(NF // 2, NF // 2)], n, 2, down)
        core_send(slot, half, up)

    def gather_core(slot, half):
        n = slot * 2 + half
        wait_bytes(g.at[slot, across, half], yr_sem.at[n * 3 + 2])
        core_send(slot, half, across)

    def project(slot, half, first, last):
        n = slot * 2 + half
        wait_bytes(g.at[slot, pl.ds(0, NY), half], cr_sem.at[n])
        left = jnp.concatenate([g[slot, p, half].reshape(HALF, HD) for p in range(NH)], axis=1)
        right = wg[slot].reshape(NH * HD, WID)
        part = jnp.dot(left, right, preferred_element_type=jnp.float32)
        rows = pl.ds(half * HALF, HALF)
        if not first:
            part = part + acc[rows]
        if last:
            out_ref[0, rows] = part.astype(jnp.bfloat16)
        else:
            acc[rows] = part

    block = 256
    per = block // POS

    def spatial(s, n):
        query = vq[head_of[spat[s]], pl.ds(pl.multiple_of(n * block, block), block)]
        return softmax_times(dot_nt(query, kv[s, 0]), kv[s, 1]).reshape(per, POS, HD)

    def spatial_b(half):
        def one(n, carry):
            g[SLOT_B, h, half, pl.ds(n * per, per)] = spatial(0, half * (HALF // block) + n)
            return carry

        lax.fori_loop(0, HALF // block, one, 0)

    def spatial_c(half):
        def one(n, carry):
            sc[half, pl.ds(n * per, per)] = spatial(1, half * (HALF // block) + n)
            return carry

        lax.fori_loop(0, HALF // block, one, 0)

    def back_a(half):
        wait_bytes(g.at[SLOT_A, h, half, pl.ds(0, NF - 1)], br_sem.at[half])
        gather_y(SLOT_A, half)

    def back_c(half):
        wait_bytes(tc.at[half, pl.ds(0, NF - 1)], br_sem.at[2 + half])
        g[SLOT_C, h, half] = jnp.where(c_temp, tc[half], sc[half])
        gather_y(SLOT_C, half)

    def sink_ready(s):
        wait_bytes(sk.at[s, pl.ds(0, NX - 1)], kr_sem.at[4 + s])
        for t in range(2):
            kv[s, t, pl.ds(TOK, TOK)] = sk[s, :, :, t].reshape(TOK, HD)

    temporal_a(0)
    send_q(0)
    send_q(1)
    sink_ready(0)
    spatial_b(0)
    gather_y(SLOT_B, 0)
    spatial_b(1)
    gather_y(SLOT_B, 1)
    temporal_a(1)
    back_a(0)
    sink_ready(1)
    spatial_c(0)
    pass_on(SLOT_B, 0)
    spatial_c(1)
    pass_on(SLOT_B, 1)
    temporal_c(0)
    gather_core(SLOT_B, 0)
    pass_on(SLOT_A, 0)
    gather_core(SLOT_B, 1)
    back_a(1)
    temporal_c(1)
    gather_core(SLOT_A, 0)
    back_c(0)
    pass_on(SLOT_A, 1)
    wait_bytes(wg.at[:, pl.ds(0, NH - 1)], wr_sem)
    project(SLOT_B, 0, True, False)
    back_c(1)
    pass_on(SLOT_C, 0)
    gather_core(SLOT_A, 1)
    project(SLOT_A, 0, False, False)
    pass_on(SLOT_C, 1)
    gather_core(SLOT_C, 0)
    project(SLOT_B, 1, True, False)
    gather_core(SLOT_C, 1)
    project(SLOT_A, 1, False, False)
    project(SLOT_C, 0, False, True)
    project(SLOT_C, 1, False, True)

    for half in range(2):
        wait_bytes(xa.at[half, pl.ds(0, NF - 1)], fs_sem.at[half])
        wait_bytes(xq.at[half, pl.ds(0, NF - 1)], fs_sem.at[3 + half])
    wait_bytes(xk.at[pl.ds(0, NF - 1)], fs_sem.at[2])
    for u in range(4):
        wait_bytes(os.at[u, pl.ds(0, NF - 1)], bs_sem.at[u])
    wait_bytes(ws.at[pl.ds(0, NH - 1)], ws_sem)
    wait_bytes(ss.at[pl.ds(0, NX - 1)], ks_sem.at[0])
    wait_bytes(qz.at[pl.ds(0, NZ - 1)], ks_sem.at[1])
    for s in range(2):
        wait_bytes(sk.at[s, 0, pl.ds(0, NZ - 1)], ks_sem.at[2 + s])
        wait_bytes(sk.at[s, pl.ds(0, NX - 1)], ks_sem.at[4 + s])
    for n in range(6):
        wait_bytes(g.at[0, pl.ds(0, NY - 1), 0], ys_sem.at[n])
        wait_bytes(g.at[0, pl.ds(0, NY), 0], cs_sem.at[n])


def per_device(queries, keys, values, out_weight, head_class, sink_frame):
    bf16, f32 = jnp.bfloat16, jnp.float32
    dma = pltpu.SemaphoreType.DMA
    spread = pltpu.VMEM
    return pl.pallas_call(
        kernel,
        out_shape=jax.ShapeDtypeStruct((1, TOK, WID), bf16),
        in_specs=[pl.BlockSpec(memory_space=pltpu.SMEM)] * 2
        + [pl.BlockSpec(memory_space=pl.ANY)] * 4,
        out_specs=pl.BlockSpec(memory_space=pltpu.VMEM),
        scratch_shapes=[
            spread((3, TOK, HD), bf16),
            spread((3, TOK, HD), bf16),
            spread((3, TOK, HD), bf16),
            spread((3, HD, NH * WID), bf16),
            spread((2, NF, 3, POS, HD), bf16),
            spread((2, NF, 3, POS, HD), bf16),
            spread((NF, 2, 2, POS, HD), bf16),
            spread((NF, 2, 2, POS, HD), bf16),
            spread((2, NF, POS, HD), bf16),
            spread((2, NF, POS, HD), bf16),
            spread((4, NF, POS, HD), bf16),
            spread((2, NF, POS, HD), bf16),
            spread((3, NH, 2, NF, POS, HD), bf16),
            spread((NH, 3, HD, WID), bf16),
            spread((3, NH, HD, WID), bf16),
            spread((TOK, WID), f32),
            spread((NX, 2, TOK // NX, HD), bf16),
            spread((NX, 2, TOK // NX, HD), bf16),
            spread((NZ, 2, TOK // NF, HD), bf16),
            spread((NZ, 2, TOK // NF, HD), bf16),
            spread((2, NX, NZ, 2, TOK // NF, HD), bf16),
            spread((2, 2, 2 * TOK, HD), bf16),
            spread((2, NF, POS, HD), bf16),
            dma((12,)),
            dma((5,)),
            dma((5,)),
            dma((4,)),
            dma((4,)),
            dma,
            dma,
            dma((6,)),
            dma((6,)),
            dma((6,)),
            dma((18,)),
            dma((6,)),
            dma((6,)),
        ],
        compiler_params=pltpu.CompilerParams(
            collective_id=0, has_side_effects=True, vmem_limit_bytes=56 * 2**20
        ),
        cost_estimate=pl.CostEstimate(
            flops=7 * 10**9, bytes_accessed=8 * 10**6, transcendentals=6 * 10**6
        ),
    )(head_class, sink_frame, queries, keys, values, out_weight)


def solution(mesh):
    placed = (
        P("frame", None, "head"),
        P("frame", None, "head"),
        P("frame", None, "head"),
        P("head", None),
        P("head"),
        P("head"),
    )
    return jax.shard_map(
        per_device, mesh=mesh, in_specs=placed, out_specs=P("frame", None, "head"), check_vma=False
    )
```

```python
import math

import jax
import jax.numpy as jnp
from jax import lax
from jax.experimental import pallas as pl
from jax.experimental.pallas import tpu as pltpu
from jax.sharding import PartitionSpec as P

MESH = pl.DeviceIdType.MESH
NX, NZ, NY, NC = 4, 8, 4, 2
NF, NH = NX * NZ, NY * NC
TOK, HD, WID = 1024, 128, 384
HALF = TOK // 2
POS = HALF // NF
SLOT_A, SLOT_C, SLOT_B = 0, 1, 2
SCALE = HD ** (-0.5) * math.log2(math.e)


def first_with(cls, kind):
    return jnp.where(cls[0] == kind, 0, jnp.where(cls[1] == kind, 1, 2))


def softmax_times(scores, values):
    top = jnp.max(scores, axis=-1, keepdims=True)
    weights = jnp.exp2((scores - top) * SCALE)
    total = jnp.sum(weights, axis=-1, keepdims=True)
    mixed = jnp.dot(weights.astype(jnp.bfloat16), values, preferred_element_type=jnp.float32)
    return (mixed / total).astype(jnp.bfloat16)


def dot_nt(a, b):
    return lax.dot_general(a, b, (((1,), (1,)), ((), ())), preferred_element_type=jnp.float32)


def kernel(
    cls,
    sink,
    q_hbm,
    k_hbm,
    v_hbm,
    w_hbm,
    out_ref,
    vq,
    vk,
    vv,
    vw,
    xa,
    ra,
    xk,
    rk,
    xq,
    rq,
    os,
    tc,
    g,
    ws,
    wg,
    acc,
    ss,
    rx,
    qz,
    rz,
    sk,
    kv,
    sc,
    in_sem,
    fs_sem,
    fr_sem,
    bs_sem,
    br_sem,
    ws_sem,
    wr_sem,
    ks_sem,
    kr_sem,
    ys_sem,
    yr_sem,
    cs_sem,
    cr_sem,
):
    f = lax.axis_index("frame")
    h = lax.axis_index("head")
    mx, mz, my, mc = f // NZ, f % NZ, h // NC, h % NC

    ins = []
    for n, (src, dst) in enumerate(((k_hbm, vk), (v_hbm, vv), (q_hbm, vq))):
        for j in range(3):
            cp = pltpu.make_async_copy(
                src.at[0, :, pl.ds(j * HD, HD)], dst.at[j], in_sem.at[n * 3 + j]
            )
            cp.start()
            ins.append(cp)
    for j in range(3):
        cp = pltpu.make_async_copy(w_hbm.at[pl.ds(j * HD, HD)], vw.at[j], in_sem.at[9 + j])
        cp.start()
        ins.append(cp)

    barrier = pltpu.get_barrier_semaphore()

    def greet_frame(d, carry):
        pl.semaphore_signal(
            barrier, inc=1, device_id=(lax.rem(f + d, NF), h), device_id_type=MESH
        )
        return carry

    def greet_head(d, carry):
        pl.semaphore_signal(
            barrier, inc=1, device_id=(f, lax.rem(h + d, NH)), device_id_type=MESH
        )
        return carry

    lax.fori_loop(1, NF, greet_frame, 0)
    lax.fori_loop(1, NH, greet_head, 0)

    ia = first_with(cls, 1)
    ib = first_with(cls, 0)
    ic = 3 - ia - ib
    c_temp = cls[ic] == 1
    head_of = {SLOT_A: ia, SLOT_B: ib, SLOT_C: ic}
    spat = (SLOT_B, SLOT_C)
    root_b, root_c = sink[ib], sink[ic]

    def wait_bytes(ref, sem):
        pltpu.make_async_copy(ref, ref, sem).wait()

    def x_peer(d):
        return lax.rem(mx + d, NX)

    def z_peer(d):
        return lax.rem(mz + d, NZ)

    def to_frames(src, dst, send_sem, recv_sem):
        def one(d, carry):
            e = NF - d
            p = lax.rem(f + lax.rem(e, 2) * ((e + 1) // 2) + (1 - lax.rem(e, 2)) * (NF - e // 2), NF)
            pltpu.make_async_remote_copy(
                src_ref=src.at[p],
                dst_ref=dst,
                send_sem=send_sem,
                recv_sem=recv_sem,
                device_id=(p, h),
                device_id_type=MESH,
            ).start()
            return carry

        lax.fori_loop(1, NF, one, 0)

    def to_x(src, dst, n):
        for d in (1, 3, 2):
            pltpu.make_async_remote_copy(
                src_ref=src(x_peer(d)),
                dst_ref=dst,
                send_sem=ks_sem.at[n],
                recv_sem=kr_sem.at[n],
                device_id=(x_peer(d) * NZ + mz, h),
                device_id_type=MESH,
            ).start()

    def to_z(src, dst, n):
        for d in (1, 7, 2, 6, 3, 5, 4):
            pltpu.make_async_remote_copy(
                src_ref=src(z_peer(d)),
                dst_ref=dst,
                send_sem=ks_sem.at[n],
                recv_sem=kr_sem.at[n],
                device_id=(mx * NZ + z_peer(d), h),
                device_id_type=MESH,
            ).start()

    for n in range(6):
        ins[n].wait()
    ss[:, 0] = vk[ib].reshape(NX, TOK // NX, HD)
    ss[:, 1] = vv[ib].reshape(NX, TOK // NX, HD)
    for t, src in enumerate((vk, vv)):
        for half in range(2):
            xk[:, t, half] = src[ic, pl.ds(half * HALF, HALF)].reshape(NF, POS, HD)
    pl.semaphore_wait(barrier, NF - 1 + NH - 1)
    to_x(lambda p: ss.at[p], rx.at[mx], 0)
    rx[mx] = ss[mx]
    rk[f] = xk[f]

    for n in range(9, 12):
        ins[n].wait()
    for slot in (SLOT_A, SLOT_C, SLOT_B):
        for p in range(NH):
            ws[p, slot] = vw[head_of[slot], :, pl.ds(p * WID, WID)]
        wg[slot, h] = ws[h, slot]

    def send_weights(d, carry):
        p = lax.rem(h + d, NH)
        pltpu.make_async_remote_copy(
            src_ref=ws.at[p],
            dst_ref=wg.at[:, h],
            send_sem=ws_sem,
            recv_sem=wr_sem,
            device_id=(f, p),
            device_id_type=MESH,
        ).start()
        return carry

    lax.fori_loop(1, NH, send_weights, 0)
    to_frames(xk, rk.at[f], fs_sem.at[2], fr_sem.at[2])

    for n in range(6, 9):
        ins[n].wait()
    for half in range(2):
        for t, src in enumerate((vq, vk, vv)):
            xa[half, :, t] = src[ia, pl.ds(half * HALF, HALF)].reshape(NF, POS, HD)
        ra[half, f] = xa[half, f]
        xq[half] = vq[ic, pl.ds(half * HALF, HALF)].reshape(NF, POS, HD)
        rq[half, f] = xq[half, f]
    for s, slot in enumerate(spat):
        kv[s, 0, pl.ds(0, TOK)] = vk[head_of[slot]]
        kv[s, 1, pl.ds(0, TOK)] = vv[head_of[slot]]

    def send_a(half):
        to_frames(xa.at[half], ra.at[half, f], fs_sem.at[half], fr_sem.at[half])

    def send_q(half):
        to_frames(xq.at[half], rq.at[half, f], fs_sem.at[3 + half], fr_sem.at[3 + half])

    wait_bytes(rx.at[pl.ds(0, NX - 1)], kr_sem.at[0])
    for t in range(2):
        qz[:, t] = rx[root_b // NZ, t].reshape(NZ, TOK // NF, HD)
    rz[mz] = qz[mz]
    to_z(lambda p: qz.at[p], rz.at[mz], 1)
    wait_bytes(rz.at[pl.ds(0, NZ - 1)], kr_sem.at[1])
    sk[0, mx, mz] = rz[root_b % NZ]
    to_z(lambda p: sk.at[0, mx, mz], sk.at[0, mx, mz], 2)
    wait_bytes(rk.at[pl.ds(0, NF - 1)], fr_sem.at[2])
    sk[1, mx, mz] = rk[root_c].reshape(2, 2 * POS, HD)
    to_z(lambda p: sk.at[1, mx, mz], sk.at[1, mx, mz], 3)
    send_a(0)
    wait_bytes(sk.at[0, 0, pl.ds(0, NZ - 1)], kr_sem.at[2])
    to_x(lambda p: sk.at[0, mx], sk.at[0, mx], 4)
    wait_bytes(sk.at[1, 0, pl.ds(0, NZ - 1)], kr_sem.at[3])
    to_x(lambda p: sk.at[1, mx], sk.at[1, mx], 5)
    send_a(1)

    def attend_positions(query, keys, values, u):
        rows = NF * POS
        query, keys, values = (a.reshape(rows, HD) for a in (query, keys, values))
        scores = dot_nt(query, keys)
        place = lax.broadcasted_iota(jnp.int32, (rows, rows), 0) % POS
        other = lax.broadcasted_iota(jnp.int32, (rows, rows), 1) % POS
        scores = jnp.where(place == other, scores, -1e30)
        os[u] = softmax_times(scores, values).reshape(NF, POS, HD)

    def temporal_a(half):
        wait_bytes(ra.at[half, pl.ds(0, NF - 1)], fr_sem.at[half])
        attend_positions(ra[half, :, 0], ra[half, :, 1], ra[half, :, 2], half)
        g[SLOT_A, h, half, f] = os[half, f]
        to_frames(os.at[half], g.at[SLOT_A, h, half, f], bs_sem.at[half], br_sem.at[half])

    def temporal_c(half):
        wait_bytes(rq.at[half, pl.ds(0, NF - 1)], fr_sem.at[3 + half])
        attend_positions(rq[half], rk[:, 0, half], rk[:, 1, half], 2 + half)
        tc[half, f] = os[2 + half, f]
        to_frames(os.at[2 + half], tc.at[half, f], bs_sem.at[2 + half], br_sem.at[2 + half])

    def core_send(slot, half, p):
        n = slot * 2 + half
        pltpu.make_async_remote_copy(
            src_ref=g.at[slot, p, half],
            dst_ref=g.at[slot, p, half],
            send_sem=cs_sem.at[n],
            recv_sem=cr_sem.at[n],
            device_id=(f, my * NC + 1 - mc),
            device_id_type=MESH,
        ).start()

    up = lax.rem(my + 1, NY) * NC + mc
    down = lax.rem(my + NY - 1, NY) * NC + mc
    across = lax.rem(my + 2, NY) * NC + mc

    def y_send(ref, n, i, p):
        pltpu.make_async_remote_copy(
            src_ref=ref,
            dst_ref=ref,
            send_sem=ys_sem.at[n],
            recv_sem=yr_sem.at[n * 3 + i],
            device_id=(f, p),
            device_id_type=MESH,
        ).start()

    def gather_y(slot, half):
        n = slot * 2 + half
        y_send(g.at[slot, h, half], n, 0, up)
        y_send(g.at[slot, h, half], n, 1, down)
        core_send(slot, half, h)

    def pass_on(slot, half):
        n = slot * 2 + half
        wait_bytes(g.at[slot, down, half], yr_sem.at[n * 3])
        y_send(g.at[slot, down, half, pl.ds(0, NF // 2)], n, 2, up)
        core_send(slot, half, down)
        wait_bytes(g.at[slot, up, half], yr_sem.at[n * 3 + 1])
        y_send(g.at[slot, up, half, pl.ds(NF // 2, NF // 2)], n, 2, down)
        core_send(slot, half, up)

    def gather_core(slot, half):
        n = slot * 2 + half
        wait_bytes(g.at[slot, across, half], yr_sem.at[n * 3 + 2])
        core_send(slot, half, across)

    def project(slot, half, first, last):
        n = slot * 2 + half
        wait_bytes(g.at[slot, pl.ds(0, NY), half], cr_sem.at[n])
        left = jnp.concatenate([g[slot, p, half].reshape(HALF, HD) for p in range(NH)], axis=1)
        right = wg[slot].reshape(NH * HD, WID)
        part = jnp.dot(left, right, preferred_element_type=jnp.float32)
        rows = pl.ds(half * HALF, HALF)
        if not first:
            part = part + acc[rows]
        if last:
            out_ref[0, rows] = part.astype(jnp.bfloat16)
        else:
            acc[rows] = part

    block = 256
    per = block // POS

    def spatial(s, n):
        query = vq[head_of[spat[s]], pl.ds(pl.multiple_of(n * block, block), block)]
        return softmax_times(dot_nt(query, kv[s, 0]), kv[s, 1]).reshape(per, POS, HD)

    def spatial_b(half):
        def one(n, carry):
            g[SLOT_B, h, half, pl.ds(n * per, per)] = spatial(0, half * (HALF // block) + n)
            return carry

        lax.fori_loop(0, HALF // block, one, 0)

    def spatial_c(half):
        def one(n, carry):
            sc[half, pl.ds(n * per, per)] = spatial(1, half * (HALF // block) + n)
            return carry

        lax.fori_loop(0, HALF // block, one, 0)

    def back_a(half):
        wait_bytes(g.at[SLOT_A, h, half, pl.ds(0, NF - 1)], br_sem.at[half])
        gather_y(SLOT_A, half)

    def back_c(half):
        wait_bytes(tc.at[half, pl.ds(0, NF - 1)], br_sem.at[2 + half])
        g[SLOT_C, h, half] = jnp.where(c_temp, tc[half], sc[half])
        gather_y(SLOT_C, half)

    def sink_ready(s):
        wait_bytes(sk.at[s, pl.ds(0, NX - 1)], kr_sem.at[4 + s])
        for t in range(2):
            kv[s, t, pl.ds(TOK, TOK)] = sk[s, :, :, t].reshape(TOK, HD)

    temporal_a(0)
    send_q(0)
    send_q(1)
    sink_ready(0)
    spatial_b(0)
    gather_y(SLOT_B, 0)
    spatial_b(1)
    gather_y(SLOT_B, 1)
    temporal_a(1)
    back_a(0)
    sink_ready(1)
    spatial_c(0)
    pass_on(SLOT_B, 0)
    spatial_c(1)
    pass_on(SLOT_B, 1)
    temporal_c(0)
    gather_core(SLOT_B, 0)
    pass_on(SLOT_A, 0)
    gather_core(SLOT_B, 1)
    back_a(1)
    temporal_c(1)
    gather_core(SLOT_A, 0)
    back_c(0)
    pass_on(SLOT_A, 1)
    wait_bytes(wg.at[:, pl.ds(0, NH - 1)], wr_sem)
    project(SLOT_B, 0, True, False)
    back_c(1)
    pass_on(SLOT_C, 0)
    gather_core(SLOT_A, 1)
    project(SLOT_A, 0, False, False)
    pass_on(SLOT_C, 1)
    gather_core(SLOT_C, 0)
    project(SLOT_B, 1, True, False)
    gather_core(SLOT_C, 1)
    project(SLOT_A, 1, False, False)
    project(SLOT_C, 0, False, True)
    project(SLOT_C, 1, False, True)

    for half in range(2):
        wait_bytes(xa.at[half, pl.ds(0, NF - 1)], fs_sem.at[half])
        wait_bytes(xq.at[half, pl.ds(0, NF - 1)], fs_sem.at[3 + half])
    wait_bytes(xk.at[pl.ds(0, NF - 1)], fs_sem.at[2])
    for u in range(4):
        wait_bytes(os.at[u, pl.ds(0, NF - 1)], bs_sem.at[u])
    wait_bytes(ws.at[pl.ds(0, NH - 1)], ws_sem)
    wait_bytes(ss.at[pl.ds(0, NX - 1)], ks_sem.at[0])
    wait_bytes(qz.at[pl.ds(0, NZ - 1)], ks_sem.at[1])
    for s in range(2):
        wait_bytes(sk.at[s, 0, pl.ds(0, NZ - 1)], ks_sem.at[2 + s])
        wait_bytes(sk.at[s, pl.ds(0, NX - 1)], ks_sem.at[4 + s])
    for n in range(6):
        wait_bytes(g.at[0, pl.ds(0, NY - 1), 0], ys_sem.at[n])
        wait_bytes(g.at[0, pl.ds(0, NY), 0], cs_sem.at[n])


def per_device(queries, keys, values, out_weight, head_class, sink_frame):
    bf16, f32 = jnp.bfloat16, jnp.float32
    dma = pltpu.SemaphoreType.DMA
    spread = pltpu.VMEM
    return pl.pallas_call(
        kernel,
        out_shape=jax.ShapeDtypeStruct((1, TOK, WID), bf16),
        in_specs=[pl.BlockSpec(memory_space=pltpu.SMEM)] * 2
        + [pl.BlockSpec(memory_space=pl.ANY)] * 4,
        out_specs=pl.BlockSpec(memory_space=pltpu.VMEM),
        scratch_shapes=[
            spread((3, TOK, HD), bf16),
            spread((3, TOK, HD), bf16),
            spread((3, TOK, HD), bf16),
            spread((3, HD, NH * WID), bf16),
            spread((2, NF, 3, POS, HD), bf16),
            spread((2, NF, 3, POS, HD), bf16),
            spread((NF, 2, 2, POS, HD), bf16),
            spread((NF, 2, 2, POS, HD), bf16),
            spread((2, NF, POS, HD), bf16),
            spread((2, NF, POS, HD), bf16),
            spread((4, NF, POS, HD), bf16),
            spread((2, NF, POS, HD), bf16),
            spread((3, NH, 2, NF, POS, HD), bf16),
            spread((NH, 3, HD, WID), bf16),
            spread((3, NH, HD, WID), bf16),
            spread((TOK, WID), f32),
            spread((NX, 2, TOK // NX, HD), bf16),
            spread((NX, 2, TOK // NX, HD), bf16),
            spread((NZ, 2, TOK // NF, HD), bf16),
            spread((NZ, 2, TOK // NF, HD), bf16),
            spread((2, NX, NZ, 2, TOK // NF, HD), bf16),
            spread((2, 2, 2 * TOK, HD), bf16),
            spread((2, NF, POS, HD), bf16),
            dma((12,)),
            dma((5,)),
            dma((5,)),
            dma((4,)),
            dma((4,)),
            dma,
            dma,
            dma((6,)),
            dma((6,)),
            dma((6,)),
            dma((18,)),
            dma((6,)),
            dma((6,)),
        ],
        compiler_params=pltpu.CompilerParams(
            collective_id=0, has_side_effects=True, vmem_limit_bytes=56 * 2**20
        ),
        cost_estimate=pl.CostEstimate(
            flops=7 * 10**9, bytes_accessed=8 * 10**6, transcendentals=6 * 10**6
        ),
    )(head_class, sink_frame, queries, keys, values, out_weight)


def solution(mesh):
    placed = (
        P("frame", None, "head"),
        P("frame", None, "head"),
        P("frame", None, "head"),
        P("head", None),
        P("head"),
        P("head"),
    )
    return jax.shard_map(
        per_device, mesh=mesh, in_specs=placed, out_specs=P("frame", None, "head"), check_vma=False
    )
```
